256 devices in a mesh: section: 8 (over z), tp: 8 (over y, core), dp: 4 (over x).
Axes of the slice: x: 4, y: 4, z: 8, core: 2. Of those that a mesh axis runs over, the one named last changes fastest.
Arguments:
- images: bfloat16 [32, 1024, 3200], P(('section', 'dp')), may hold values from -6 to 6
- counts: int32 [32], P(('section', 'dp')), may hold values from 256 to 1024, as said below
- norm_gain: float32 [3200], replicated, may hold values from 0.25 to 1.75
- w_qkv: bfloat16 [3, 3200, 3072], P(None, ('section', 'dp'), 'tp'), may hold values from -1 to 1
- w_out: bfloat16 [3072, 3200], P('tp', ('section', 'dp')), may hold values from -1 to 1
- layer_scale: float32 [3200], P('tp'), may hold values from 0.5 to 1.5
- order: int32 [4, 8], replicated, may hold values from 0 to 7, each once within a row
Outputs:
- vision_tokens: bfloat16 [4, 8, 1024, 3200], P('dp', None, 'section', 'tp')
The draws below stay inside these ranges and needn't reach their ends.
Inputs may be any that keep to these rules, and one draw needn't show every extreme that they name: `counts`: some block in every draw is full. `order`: each row is a permutation.
All inputs are finite; a program needn't handle non-finite values.
Results may differ from the reference program's by a relative error of at most 0.02.
Values may be sent and summed in bfloat16 or wider, within the bound.
No kernel may reach another device: no remote copies, remote signals or barrier semaphores. Data moves between devices by JAX's collectives and lax.ppermute only.
A program may use at most 128 MiB of HBM per device.

```python
import math
import jax
import jax.numpy as jnp
from jax import lax

D = 3200
HD = 128
HEADS_DEV = 3
HEADS = 24
BLOCK = 1024
BLOCKS = 32
N_SECTION = 8
N_TP = 8
N_DP = 4


def draw_counts(key, part):
    key = jax.random.fold_in(key, 7)
    first, second = jax.random.split(key)
    values = jax.random.randint(first, (BLOCKS,), BLOCK // 4, BLOCK + 1)
    where = jax.random.randint(second, (), 0, BLOCKS)
    return values.at[where].set(BLOCK).astype(jnp.int32)


def draw_images(key, part):
    key = jax.random.fold_in(key, 11)
    drawn = jnp.clip(jax.random.normal(key, (BLOCKS, BLOCK, D), jnp.float32), -6.0, 6.0)
    return drawn.astype(jnp.bfloat16)


def draw_w_qkv(key, part):
    key = jax.random.fold_in(key, 13)
    key_base = jax.random.fold_in(key, 0)
    drawn = jnp.clip(jax.random.normal(key_base, (3, D, HEADS * HD), jnp.float32), -6.0, 6.0) * D ** (-0.5)
    return drawn.astype(jnp.bfloat16)


def steps_of(key, dims, pieces, low, high):
    level = 1.0
    for position, shards_of in pieces:
        draws = jax.random.uniform(jax.random.fold_in(jax.random.fold_in(key, 6), position), (shards_of,), jnp.float32, low / len(pieces), high / len(pieces))
        level = level * jnp.repeat(jnp.exp(draws), dims[position] // shards_of).reshape((-1,) + (1,) * (len(dims) - 1 - position))
    return level


def bell_draw(key, dims, deviation, most, shards=(), held_as=jnp.bfloat16):
    entries = deviation * jax.random.normal(key, dims, jnp.float32)
    if shards:
        entries = entries * steps_of(key, dims, shards, -0.22, 0.18)
    return jnp.clip(entries, -most, most).astype(held_as)


def setup_inputs(seed: int = 0) -> dict:
    keys = jax.random.split(jax.random.key(seed), 8)
    images = draw_images(jax.random.fold_in(keys[7], 71), 0)
    counts = draw_counts(jax.random.fold_in(keys[7], 71), 0)
    norm_gain = jnp.clip(1.0 + 0.15 * jax.random.normal(keys[2], (D,), jnp.float32), 0.25, 1.75)
    w_qkv = draw_w_qkv(jax.random.fold_in(keys[7], 71), 0)
    w_out = bell_draw(keys[4], (HEADS * HD, D), (HD // 4) ** -0.5, 1.0, ((0, 8), (1, 32)))
    layer_scale = jnp.clip(0.5 + 1.0 * jax.random.uniform(keys[5], (D,), jnp.float32) ** steps_of(keys[5], (D,), ((0, 8),), -0.2, 0.2), 0.5, 1.5)
    order = jax.vmap(lambda own: jax.random.permutation(own, N_SECTION))(jax.random.split(keys[6], N_DP)).reshape((N_DP, N_SECTION)).astype(jnp.int32)
    return {"images": images, "counts": counts, "norm_gain": norm_gain, "w_qkv": w_qkv, "w_out": w_out, "layer_scale": layer_scale, "order": order}


def encode_block(block, count, norm_gain, w_qkv, w_out, layer_scale):
    x = block.astype(jnp.float32)
    normed = (x * lax.rsqrt(lax.optimization_barrier(jnp.mean(x * x, axis=-1, keepdims=True)) + 1e-06) * norm_gain).astype(jnp.bfloat16)
    projections = jnp.einsum('rd,tdc->trc', normed.astype(jnp.float32), w_qkv.astype(jnp.float32)).astype(jnp.bfloat16)
    query = projections[0].reshape(BLOCK, HEADS, HD).astype(jnp.float32)
    key = projections[1].reshape(BLOCK, HEADS, HD).astype(jnp.float32)
    value = projections[2].reshape(BLOCK, HEADS, HD).astype(jnp.float32)
    scores = jnp.einsum('rhe,jhe->hrj', query, key) / math.sqrt(HD)
    valid = jnp.arange(BLOCK, dtype=jnp.int32) < count
    scores = jnp.where(valid[None, None, :], scores, -jnp.inf)
    top = lax.optimization_barrier(jnp.max(scores, axis=-1, keepdims=True))
    expo = jnp.exp(scores - top)
    probs = (expo / lax.optimization_barrier(jnp.sum(expo, axis=-1, keepdims=True))).astype(jnp.bfloat16)
    context = jnp.einsum('hrj,jhe->rhe', probs.astype(jnp.float32), value).astype(jnp.bfloat16)
    context = context.reshape(BLOCK, N_TP, HEADS_DEV * HD).astype(jnp.float32)
    weights = w_out.reshape(N_TP, HEADS_DEV * HD, D).astype(jnp.float32)
    partial_value = jnp.einsum('rgc,gcd->grd', context, weights).astype(jnp.bfloat16)
    projected = lax.optimization_barrier(jnp.sum(partial_value.astype(jnp.float32), axis=0))
    rows = jnp.arange(BLOCK, dtype=jnp.int32) < count
    encoded = jnp.where(rows[:, None], x + layer_scale * projected, 0.0)
    return encoded.astype(jnp.bfloat16)

def reference(images, counts, norm_gain, w_qkv, w_out, layer_scale, order):
    encoded = lax.map(lambda pair: encode_block(pair[0], pair[1], norm_gain, w_qkv, w_out, layer_scale), (images, counts))
    per_replica = jnp.transpose(encoded.reshape(N_SECTION, N_DP, BLOCK, D), (1, 0, 2, 3))
    return jax.vmap(lambda blocks, slots: jnp.take(blocks, slots, axis=0))(per_replica, order)
```

```python
import math

import jax
import jax.numpy as jnp
from jax import lax
from jax.experimental import pallas as pl
from jax.experimental.pallas import tpu as pltpu
from jax.sharding import PartitionSpec as P

HD = 128
BF = jnp.bfloat16
F32 = jnp.float32
ORDER = (4, 3, 5, 2, 6, 1, 7, 0)
GROUPS = ((0, 4), (4, 8))
TILE = 256


def norm_body(x_ref, gain_ref, by_section, by_dp):
    x = x_ref[...].astype(F32)
    scale = lax.rsqrt(jnp.mean(x * x, axis=-1, keepdims=True) + 1e-06)
    y = (x * scale * gain_ref[...]).astype(BF)
    for s in range(8):
        by_section[s] = y[:, s * 400 : s * 400 + 400]
        for d in range(4):
            piece = y[:, (s * 4 + d) * 100 : (s * 4 + d) * 100 + 100]
            by_dp[d * 2 + s // 4, :, (s % 4) * 100 : (s % 4) * 100 + 100] = piece


def normalise(x, gain):
    rows, wide = x.shape
    tile = 128
    return pl.pallas_call(
        norm_body,
        grid=(rows // tile,),
        in_specs=[
            pl.BlockSpec((tile, wide), lambda r: (r, 0)),
            pl.BlockSpec((1, wide), lambda r: (0, 0)),
        ],
        out_specs=[
            pl.BlockSpec((8, tile, 400), lambda r: (0, r, 0)),
            pl.BlockSpec((8, tile, 400), lambda r: (0, r, 0)),
        ],
        out_shape=[jax.ShapeDtypeStruct((8, rows, 400), BF)] * 2,
        compiler_params=pltpu.CompilerParams(vmem_limit_bytes=24 * 2**20),
        cost_estimate=pl.CostEstimate(flops=30_000_000, bytes_accessed=20_000_000, transcendentals=1024),
    )(x, gain[None])


def attend_body(count_ref, q_ref, k_ref, vt_ref, out_ref):
    keys = k_ref.shape[0]
    rows = q_ref.shape[0]
    live = lax.broadcasted_iota(jnp.int32, (keys, rows), 0) < count_ref[0]
    factor = math.log2(math.e) / math.sqrt(HD)
    for h in range(q_ref.shape[1] // HD):
        at = slice(h * HD, h * HD + HD)
        scores = lax.dot_general(
            k_ref[:, at], q_ref[:, at], (((1,), (1,)), ((), ())), preferred_element_type=F32
        )
        scores = jnp.where(live, scores, -jnp.inf)
        top = jnp.max(scores, axis=0, keepdims=True)
        expo = jnp.exp2((scores - top) * factor)
        total = jnp.sum(expo, axis=0, keepdims=True)
        context = jnp.dot(vt_ref[at, :], expo.astype(BF), preferred_element_type=F32)
        context = (context / total).astype(BF)
        for j in range(rows // 128):
            out_ref[j, at, :] = context[:, j * 128 : j * 128 + 128]


def attend(count, q, k, vt):
    rows, wide = q.shape
    keys = k.shape[0]
    return pl.pallas_call(
        attend_body,
        grid_spec=pltpu.PrefetchScalarGridSpec(
            num_scalar_prefetch=1,
            grid=(rows // TILE,),
            in_specs=[
                pl.BlockSpec((TILE, wide), lambda r, c: (r, 0)),
                pl.BlockSpec((keys, wide), lambda r, c: (0, 0)),
                pl.BlockSpec((wide, keys), lambda r, c: (0, 0)),
            ],
            out_specs=pl.BlockSpec((TILE // 128, wide, 128), lambda r, c: (r, 0, 0)),
        ),
        out_shape=jax.ShapeDtypeStruct((rows // 128, wide, 128), BF),
        compiler_params=pltpu.CompilerParams(vmem_limit_bytes=24 * 2**20),
        cost_estimate=pl.CostEstimate(
            flops=4 * rows * keys * wide, bytes_accessed=4_000_000, transcendentals=rows * keys * 3
        ),
    )(count, q, k, vt)


def project_body(info_ref, a0, a1, a2, a3, b_ref, w_ref, own_ref, scale_ref, out_ref):
    chunk = pl.program_id(0)
    total = None
    for j in range(8):
        ctx = (a0, a1, a2, a3)[j][0] if j < 4 else b_ref[j - 4, 0]
        term = jnp.dot(w_ref[info_ref[j]], ctx, preferred_element_type=F32)
        total = term if total is None else total + term
    row = lax.broadcasted_iota(jnp.int32, (1, 128), 1) + info_ref[9 + chunk]
    value = own_ref[0].astype(F32) + scale_ref[...] * total
    out_ref[0] = jnp.where(row < info_ref[8], value, 0.0).astype(BF)


def project(info, near, sibling, w8, own, scale):
    chunks = own.shape[0]
    tall, deep = w8.shape[1:]
    one = pl.BlockSpec((1, deep, 128), lambda c, i: (c, 0, 0))
    return pl.pallas_call(
        project_body,
        grid_spec=pltpu.PrefetchScalarGridSpec(
            num_scalar_prefetch=1,
            grid=(chunks,),
            in_specs=[
                one, one, one, one,
                pl.BlockSpec((4, 1, deep, 128), lambda c, i: (0, c, 0, 0)),
                pl.BlockSpec((8, tall, deep), lambda c, i: (0, 0, 0)),
                pl.BlockSpec((1, tall, 128), lambda c, i: (c, 0, 0)),
                pl.BlockSpec((tall, 1), lambda c, i: (0, 0)),
            ],
            out_specs=pl.BlockSpec((1, tall, 128), lambda c, i: (c, 0, 0)),
        ),
        out_shape=jax.ShapeDtypeStruct((chunks, tall, 128), BF),
        compiler_params=pltpu.CompilerParams(vmem_limit_bytes=24 * 2**20),
        cost_estimate=pl.CostEstimate(
            flops=2 * chunks * tall * deep * 8 * 128, bytes_accessed=6_000_000, transcendentals=0
        ),
    )(info, *near, sibling, w8, own, scale)


def around(x, axis, step, size):
    return lax.ppermute(x, axis, [(i, (i + step) % size) for i in range(size)])


def place(parts, places, count):
    out = jnp.zeros((count,) + parts[0].shape, parts[0].dtype)
    for part, at in zip(parts, places):
        out = lax.dynamic_update_slice(out, part[None], (at, 0, 0))
    return out.reshape(count * parts[0].shape[0], parts[0].shape[1])


def pick(array, at):
    return lax.dynamic_index_in_dim(array, at, 0, keepdims=False)


def ring(block, axis, size, use):
    use(0, block)
    right, left = block, block
    for step in range(1, size // 2):
        right = around(right, axis, 1, size)
        left = around(left, axis, -1, size)
        use(-step, right)
        use(step, left)
    half = block.shape[0] // 2
    top = around(right[:half], axis, 1, size)
    low = around(left[half:], axis, -1, size)
    return top, low


def shards(images, counts, norm_gain, w_qkv, w_out, layer_scale, order):
    sec, tp, dp = (lax.axis_index(a) for a in ("section", "tp", "dp"))
    y, core = tp // 2, tp % 2
    whole = images[0]
    count = counts[0]
    share = layer_scale.shape[0]

    w_o = lax.ppermute(
        w_out.T, ("section", "tp"), [(s * 8 + t, t * 8 + s) for s in range(8) for t in range(8)]
    )
    w_b = jnp.concatenate([w_qkv[0], w_qkv[1]], axis=1)
    w_v = w_qkv[2]

    def over_dp(x):
        back = around(x, "dp", 1, 4)
        ahead = around(x, "dp", -1, 4)
        far = around(x, "dp", 2, 4)
        return place((x, back, ahead, far), (dp, (dp + 3) % 4, (dp + 1) % 4, (dp + 2) % 4), 4)

    got = {}
    top, low = ring(w_b, "section", 8, got.__setitem__)
    parts = [got[k] for k in (0, -1, 1, -2, 2, -3, 3)] + [jnp.concatenate([top, low], axis=0)]
    places = [(sec + k) % 8 for k in (0, 7, 1, 6, 2, 5, 3, 4)]
    block_b = place(parts, places, 8)
    block_v = over_dp(w_v)
    block_o = over_dp(w_o)
    w8 = lax.all_gather(block_o, "section", axis=0, tiled=False)

    by_section, by_dp = normalise(whole, norm_gain)
    sums = {"v": None, "b": None}

    def add(name, left, right):
        term = jnp.dot(left, right, preferred_element_type=F32)
        sums[name] = term if sums[name] is None else sums[name] + term

    def use_v(distance, block):
        add("v", pick(by_section, (sec + distance + 8) % 8), block)

    def use_b(distance, block):
        at = (dp + distance + 4) % 4
        add("b", pick(by_dp, at * 2), block[:400])
        add("b", pick(by_dp, at * 2 + 1), block[400:])

    top_b, low_b = ring(block_b, "dp", 4, use_b)
    far = (dp + 2) % 4
    add("b", pick(by_dp, far * 2), top_b)
    add("b", pick(by_dp, far * 2 + 1), low_b)
    top_v, low_v = ring(block_v, "section", 8, use_v)
    use_v(4, jnp.concatenate([top_v, low_v], axis=0))

    both = sums["b"].astype(BF)
    query, key = both[:, :384], both[:, 384:]
    value_t = sums["v"].astype(BF).T

    rel = (sec + jnp.array(ORDER, jnp.int32)) % 8
    query = jnp.take(query.reshape(8, 128, 384), rel, axis=0, mode="clip").reshape(1024, 384)
    own = lax.dynamic_slice_in_dim(whole, tp * share, share, 1)
    own = jnp.take(own.reshape(8, 128, share).transpose(0, 2, 1), rel, axis=0, mode="clip")
    near_groups = [2 * ((y + off) % 4) + core for off in (0, 3, 1, 2)]
    far_groups = [2 * ((y + off) % 4) + 1 - core for off in (0, 3, 1, 2)]
    scale = layer_scale[:, None]

    received = {}
    for first, last in GROUPS:
        ctx = attend(counts, query[first * 128 : last * 128], key, value_t)
        back = around(ctx, "tp", 2, 8)
        ahead = around(ctx, "tp", -2, 8)
        half = (last - first) // 2
        top = around(back[:half], "tp", 2, 8)
        low = around(ahead[half:], "tp", -2, 8)
        near = (ctx, back, ahead, jnp.concatenate([top, low], axis=0))
        sibling = lax.ppermute(jnp.stack(near), "tp", [(i, i ^ 1) for i in range(8)])
        info = jnp.stack(near_groups + far_groups + [count]).astype(jnp.int32)
        info = jnp.concatenate([info, rel[first:last] * 128])
        encoded = project(info, near, sibling, w8, own[first:last], scale)
        for j in range(first, last):
            k = ORDER[j]
            piece = encoded[j - first]
            received[k] = around(piece, "section", k, 8) if k else piece

    stack = jnp.stack([received[k] for k in range(8)])
    slots = pick(order, dp)
    arranged = jnp.take(stack, (sec - slots + 8) % 8, axis=0, mode="clip")
    return arranged.transpose(0, 2, 1)[None]


def solution(mesh):
    in_specs = (
        P(("section", "dp"), None, None),
        P(("section", "dp")),
        P(),
        P(None, ("section", "dp"), "tp"),
        P("tp", ("section", "dp")),
        P("tp"),
        P(),
    )
    out_specs = P("dp", None, "section", "tp")
    return jax.shard_map(shards, mesh=mesh, in_specs=in_specs, out_specs=out_specs, check_vma=False)
```

```python
import math

import jax
import jax.numpy as jnp
from jax import lax
from jax.experimental import pallas as pl
from jax.experimental.pallas import tpu as pltpu
from jax.sharding import PartitionSpec as P

HD = 128
BF = jnp.bfloat16
F32 = jnp.float32
ORDER = (4, 3, 5, 2, 6, 1, 7, 0)
GROUPS = ((0, 4), (4, 8))
TILE = 256


def norm_body(x_ref, gain_ref, plain, by_dp):
    x = x_ref[...].astype(F32)
    scale = lax.rsqrt(jnp.mean(x * x, axis=-1, keepdims=True) + 1e-06)
    y = (x * scale * gain_ref[...]).astype(BF)
    plain[...] = y
    for s in range(8):
        for d in range(4):
            by_dp[d, :, s * 100 : s * 100 + 100] = y[:, (s * 4 + d) * 100 : (s * 4 + d) * 100 + 100]


def normalise(x, gain):
    rows, wide = x.shape
    tile = 128
    return pl.pallas_call(
        norm_body,
        grid=(rows // tile,),
        in_specs=[
            pl.BlockSpec((tile, wide), lambda r: (r, 0)),
            pl.BlockSpec((1, wide), lambda r: (0, 0)),
        ],
        out_specs=[
            pl.BlockSpec((tile, wide), lambda r: (r, 0)),
            pl.BlockSpec((4, tile, 800), lambda r: (0, r, 0)),
        ],
        out_shape=[
            jax.ShapeDtypeStruct((rows, wide), BF),
            jax.ShapeDtypeStruct((4, rows, 800), BF),
        ],
        compiler_params=pltpu.CompilerParams(vmem_limit_bytes=16 * 2**20),
        cost_estimate=pl.CostEstimate(flops=30_000_000, bytes_accessed=20_000_000, transcendentals=1024),
    )(x, gain[None])


def attend_body(count_ref, q_ref, k_ref, vt_ref, out_ref):
    keys = k_ref.shape[0]
    rows = q_ref.shape[0]
    live = lax.broadcasted_iota(jnp.int32, (keys, rows), 0) < count_ref[0]
    factor = math.log2(math.e) / math.sqrt(HD)
    for h in range(q_ref.shape[1] // HD):
        at = slice(h * HD, h * HD + HD)
        scores = lax.dot_general(
            k_ref[:, at], q_ref[:, at], (((1,), (1,)), ((), ())), preferred_element_type=F32
        )
        scores = jnp.where(live, scores, -jnp.inf)
        top = jnp.max(scores, axis=0, keepdims=True)
        expo = jnp.exp2((scores - top) * factor)
        total = jnp.sum(expo, axis=0, keepdims=True)
        context = jnp.dot(vt_ref[at, :], expo.astype(BF), preferred_element_type=F32)
        out_ref[at, :] = (context / total).astype(BF)


def attend(count, q, k, vt):
    rows, wide = q.shape
    keys = k.shape[0]
    return pl.pallas_call(
        attend_body,
        grid_spec=pltpu.PrefetchScalarGridSpec(
            num_scalar_prefetch=1,
            grid=(rows // TILE,),
            in_specs=[
                pl.BlockSpec((TILE, wide), lambda r, c: (r, 0)),
                pl.BlockSpec((keys, wide), lambda r, c: (0, 0)),
                pl.BlockSpec((wide, keys), lambda r, c: (0, 0)),
            ],
            out_specs=pl.BlockSpec((wide, TILE), lambda r, c: (0, r)),
        ),
        out_shape=jax.ShapeDtypeStruct((wide, rows), BF),
        compiler_params=pltpu.CompilerParams(vmem_limit_bytes=24 * 2**20),
        cost_estimate=pl.CostEstimate(
            flops=4 * rows * keys * wide, bytes_accessed=4_000_000, transcendentals=rows * keys * 3
        ),
    )(count, q, k, vt)


def project_body(info_ref, own_ctx, back, ahead, far, sibling, w_ref, own_ref, scale_ref, out_ref):
    near = (own_ctx, back, ahead, far)
    total = None
    for j in range(8):
        ctx = near[j][...] if j < 4 else sibling[j - 4]
        term = jnp.dot(w_ref[info_ref[j]], ctx, preferred_element_type=F32)
        total = term if total is None else total + term
    total = scale_ref[...] * total
    for c in range(out_ref.shape[0]):
        row = lax.broadcasted_iota(jnp.int32, (1, 128), 1) + info_ref[9 + c]
        value = own_ref[c].astype(F32) + total[:, c * 128 : c * 128 + 128]
        out_ref[c] = jnp.where(row < info_ref[8], value, 0.0).astype(BF)


def project(info, near, sibling, w8, own, scale):
    chunks, tall = own.shape[:2]
    whole = pl.BlockSpec(memory_space=pltpu.VMEM)
    return pl.pallas_call(
        project_body,
        in_specs=[pl.BlockSpec(memory_space=pltpu.SMEM)] + [whole] * 8,
        out_specs=whole,
        out_shape=jax.ShapeDtypeStruct((chunks, tall, 128), BF),
        compiler_params=pltpu.CompilerParams(vmem_limit_bytes=24 * 2**20),
        cost_estimate=pl.CostEstimate(
            flops=2 * chunks * tall * 384 * 8 * 128, bytes_accessed=6_000_000, transcendentals=0
        ),
    )(info, *near, sibling, w8, own, scale)


def around(x, axis, step, size):
    return lax.ppermute(x, axis, [(i, (i + step) % size) for i in range(size)])


def place(parts, places, count):
    out = jnp.zeros((count,) + parts[0].shape, parts[0].dtype)
    for part, at in zip(parts, places):
        out = lax.dynamic_update_slice(out, part[None], (at, 0, 0))
    return out.reshape(count * parts[0].shape[0], parts[0].shape[1])


def pick(array, at):
    return lax.dynamic_index_in_dim(array, at, 0, keepdims=False)


def shards(images, counts, norm_gain, w_qkv, w_out, layer_scale, order):
    sec, tp, dp = (lax.axis_index(a) for a in ("section", "tp", "dp"))
    y, core = tp // 2, tp % 2
    whole = images[0]
    count = counts[0]
    share = layer_scale.shape[0]

    w_b = jnp.concatenate([w_qkv[0], w_qkv[1]], axis=1)
    block_b = lax.all_gather(w_b, "section", axis=0, tiled=False).reshape(800, 768)

    w_o = lax.ppermute(
        w_out.T, ("section", "tp"), [(s * 8 + t, t * 8 + s) for s in range(8) for t in range(8)]
    )
    w_a = jnp.concatenate([w_qkv[2], w_o], axis=1)
    parts = (w_a, around(w_a, "dp", 1, 4), around(w_a, "dp", -1, 4), around(w_a, "dp", 2, 4))
    block_a = place(parts, (dp, (dp + 3) % 4, (dp + 1) % 4, (dp + 2) % 4), 4)
    w_v = lax.all_gather(block_a[:, :384], "section", axis=0, tiled=True)
    block_o, _ = lax.optimization_barrier((block_a[:, 384:], w_v))
    w8 = lax.all_gather(block_o, "section", axis=0, tiled=False)

    normed, by_dp = normalise(whole, norm_gain)

    back_top = around(block_b[:400], "dp", 1, 4)
    ahead_low = around(block_b[400:], "dp", -1, 4)
    back_low = around(block_b[400:], "dp", 1, 4)
    ahead_top = around(block_b[:400], "dp", -1, 4)
    far_top = around(back_top, "dp", 1, 4)
    far_low = around(ahead_low, "dp", -1, 4)

    def dot(left, right):
        return jnp.dot(left, right, preferred_element_type=F32)

    both = dot(pick(by_dp, dp), block_b)
    both = both + dot(pick(by_dp, (dp + 3) % 4), jnp.concatenate([back_top, back_low], axis=0))
    both = both + dot(pick(by_dp, (dp + 1) % 4), jnp.concatenate([ahead_top, ahead_low], axis=0))
    both = both + dot(pick(by_dp, (dp + 2) % 4), jnp.concatenate([far_top, far_low], axis=0))
    both = both.astype(BF)
    query, key = both[:, :384], both[:, 384:]
    value_t = dot(normed, w_v).astype(BF).T

    rel = (sec + jnp.array(ORDER, jnp.int32)) % 8
    query = jnp.take(query.reshape(8, 128, 384), rel, axis=0, mode="clip").reshape(1024, 384)
    own = lax.dynamic_slice_in_dim(whole, tp * share, share, 1)
    own = jnp.take(own.reshape(8, 128, share).transpose(0, 2, 1), rel, axis=0, mode="clip")
    near_groups = [2 * ((y + off) % 4) + core for off in (0, 3, 1, 2)]
    far_groups = [2 * ((y + off) % 4) + 1 - core for off in (0, 3, 1, 2)]
    scale = layer_scale[:, None]

    received = {}
    for first, last in GROUPS:
        ctx = attend(counts, query[first * 128 : last * 128], key, value_t)
        back = around(ctx, "tp", 2, 8)
        ahead = around(ctx, "tp", -2, 8)
        half = ctx.shape[0] // 2
        top = around(back[:half], "tp", 2, 8)
        low = around(ahead[half:], "tp", -2, 8)
        near = (ctx, back, ahead, jnp.concatenate([top, low], axis=0))
        sibling = lax.ppermute(jnp.stack(near), "tp", [(i, i ^ 1) for i in range(8)])
        info = jnp.stack(near_groups + far_groups + [count]).astype(jnp.int32)
        info = jnp.concatenate([info, rel[first:last] * 128])
        encoded = project(info, near, sibling, w8, own[first:last], scale)
        for j in range(first, last):
            k = ORDER[j]
            piece = encoded[j - first]
            received[k] = around(piece, "section", k, 8) if k else piece

    stack = jnp.stack([received[k] for k in range(8)])
    slots = pick(order, dp)
    arranged = jnp.take(stack, (sec - slots + 8) % 8, axis=0, mode="clip")
    return arranged.transpose(0, 2, 1)[None]


def solution(mesh):
    in_specs = (
        P(("section", "dp"), None, None),
        P(("section", "dp")),
        P(),
        P(None, ("section", "dp"), "tp"),
        P("tp", ("section", "dp")),
        P("tp"),
        P(),
    )
    out_specs = P("dp", None, "section", "tp")
    return jax.shard_map(shards, mesh=mesh, in_specs=in_specs, out_specs=out_specs, check_vma=False)
```

```python
import functools
import math

import jax
import jax.numpy as jnp
from jax import lax
from jax.experimental import pallas as pl
from jax.experimental.pallas import tpu as pltpu
from jax.sharding import PartitionSpec as P

HD = 128
BF = jnp.bfloat16
F32 = jnp.float32
ORDER = (4, 3, 5, 2, 6, 1, 7, 0)
GROUPS = ((0, 4), (4, 8))


def norm_body(x_ref, gain_ref, plain, by_dp):
    x = x_ref[...].astype(F32)
    scale = lax.rsqrt(jnp.mean(x * x, axis=-1, keepdims=True) + 1e-06)
    y = (x * scale * gain_ref[...]).astype(BF)
    plain[...] = y
    for s in range(8):
        for d in range(4):
            by_dp[d, :, s * 100 : s * 100 + 100] = y[:, (s * 4 + d) * 100 : (s * 4 + d) * 100 + 100]


def normalise(x, gain):
    rows, wide = x.shape
    tile = 128
    return pl.pallas_call(
        norm_body,
        grid=(rows // tile,),
        in_specs=[
            pl.BlockSpec((tile, wide), lambda r: (r, 0)),
            pl.BlockSpec((1, wide), lambda r: (0, 0)),
        ],
        out_specs=[
            pl.BlockSpec((tile, wide), lambda r: (r, 0)),
            pl.BlockSpec((4, tile, 800), lambda r: (0, r, 0)),
        ],
        out_shape=[
            jax.ShapeDtypeStruct((rows, wide), BF),
            jax.ShapeDtypeStruct((4, rows, 800), BF),
        ],
        compiler_params=pltpu.CompilerParams(vmem_limit_bytes=16 * 2**20),
        cost_estimate=pl.CostEstimate(flops=30_000_000, bytes_accessed=20_000_000, transcendentals=1024),
    )(x, gain[None])


def early_body(at_ref, x_ref, own_top, own_low, back_top, back_low, ahead_top, ahead_low, out_ref):
    total = jnp.zeros(out_ref.shape, F32)
    for k, (top, low) in enumerate(((own_top, own_low), (back_top, back_low), (ahead_top, ahead_low))):
        total += jnp.dot(x_ref[at_ref[k], :, :400], top[...], preferred_element_type=F32)
        total += jnp.dot(x_ref[at_ref[k], :, 400:], low[...], preferred_element_type=F32)
    out_ref[...] = total


def early(at, by_dp, *halves):
    rows, deep = by_dp.shape[1:]
    wide = halves[0].shape[1]
    tile = 256
    half = pl.BlockSpec((deep // 2, wide), lambda r, a: (0, 0))
    return pl.pallas_call(
        early_body,
        grid_spec=pltpu.PrefetchScalarGridSpec(
            num_scalar_prefetch=1,
            grid=(rows // tile,),
            in_specs=[
                pl.BlockSpec((4, tile, deep), lambda r, a: (0, r, 0)),
            ]
            + [half] * 6,
            out_specs=pl.BlockSpec((tile, wide), lambda r, a: (r, 0)),
        ),
        out_shape=jax.ShapeDtypeStruct((rows, wide), F32),
        compiler_params=pltpu.CompilerParams(vmem_limit_bytes=58 * 2**20),
        cost_estimate=pl.CostEstimate(
            flops=6 * rows * deep * wide, bytes_accessed=15_000_000, transcendentals=0
        ),
    )(at, by_dp, *halves)


def attend_tile(live_keys, query, key, vt, out_ref):
    keys = key.shape[0]
    rows = query.shape[0]
    live = lax.broadcasted_iota(jnp.int32, (keys, rows), 0) < live_keys
    factor = math.log2(math.e) / math.sqrt(HD)
    for h in range(out_ref.shape[0] // HD):
        at = slice(h * HD, h * HD + HD)
        scores = lax.dot_general(
            key[:, at], query[:, at], (((1,), (1,)), ((), ())), preferred_element_type=F32
        )
        scores = jnp.where(live, scores, -jnp.inf)
        top = jnp.max(scores, axis=0, keepdims=True)
        expo = jnp.exp2((scores - top) * factor)
        total = jnp.sum(expo, axis=0, keepdims=True)
        context = jnp.dot(vt[at, :], expo.astype(BF), preferred_element_type=F32)
        out_ref[at, :] = (context / total).astype(BF)


def late_body(at_ref, sums, x_ref, top, low, normed, w_ref, qk_ref, vt_ref, ctx_ref, qk, vt):
    step = pl.program_id(0)
    tile, wide = sums.shape
    narrow = wide // 2

    @pl.when(step < 4)
    def _():
        total = sums[...] + jnp.dot(x_ref[0, :, :400], top[...], preferred_element_type=F32)
        total += jnp.dot(x_ref[0, :, 400:], low[...], preferred_element_type=F32)
        qk_ref[...] = total.astype(BF)
        value = jnp.dot(normed[...], w_ref[...], preferred_element_type=F32)
        vt_ref[...] = value.T.astype(BF)

    for r in range(4):

        @pl.when(step == r)
        def _():
            qk[r * tile : r * tile + tile] = qk_ref[...]
            vt[:, r * tile : r * tile + tile] = vt_ref[...]

    @pl.when(step >= 4)
    def _():
        rows = [
            pl.ds(pl.multiple_of(at_ref[5 + 2 * (step - 4) + i] * 128, 128), 128) for i in range(2)
        ]
        query = jnp.concatenate([qk[rows[0], :narrow], qk[rows[1], :narrow]], axis=0)
        attend_tile(at_ref[4], query, qk[:, narrow:], vt, ctx_ref)


def late(at, sums, by_dp, top, low, normed, w_v):
    rows, wide = sums.shape
    deep, tall = by_dp.shape[2], normed.shape[1]
    narrow = w_v.shape[1]
    tile = rows // 4
    half = pl.BlockSpec((deep // 2, wide), lambda r, a: (0, 0))

    def upto(r):
        return jnp.minimum(r, 3)

    return pl.pallas_call(
        late_body,
        grid_spec=pltpu.PrefetchScalarGridSpec(
            num_scalar_prefetch=1,
            grid=(6,),
            in_specs=[
                pl.BlockSpec((tile, wide), lambda r, a: (upto(r), 0)),
                pl.BlockSpec((1, tile, deep), lambda r, a: (a[3], upto(r), 0)),
                half,
                half,
                pl.BlockSpec((tile, tall), lambda r, a: (upto(r), 0)),
                pl.BlockSpec((tall, narrow), lambda r, a: (0, 0)),
            ],
            out_specs=[
                pl.BlockSpec((tile, wide), lambda r, a: (upto(r), 0)),
                pl.BlockSpec((narrow, tile), lambda r, a: (0, upto(r))),
                pl.BlockSpec((narrow, 256), lambda r, a: (0, jnp.maximum(r - 4, 0))),
            ],
            scratch_shapes=[pltpu.VMEM((rows, wide), BF), pltpu.VMEM((narrow, rows), BF)],
        ),
        out_shape=[
            jax.ShapeDtypeStruct((rows, wide), BF),
            jax.ShapeDtypeStruct((narrow, rows), BF),
            jax.ShapeDtypeStruct((narrow, 512), BF),
        ],
        compiler_params=pltpu.CompilerParams(vmem_limit_bytes=58 * 2**20),
        cost_estimate=pl.CostEstimate(
            flops=2 * rows * (deep * wide + tall * narrow) + 2 * rows * rows * narrow,
            bytes_accessed=18_000_000,
            transcendentals=rows * rows * 3 // 2,
        ),
    )(at, sums, by_dp, top, low, normed, w_v)


def attend_body(info_ref, q0_ref, q1_ref, k_ref, vt_ref, out_ref):
    query = jnp.concatenate([q0_ref[...], q1_ref[...]], axis=0)
    attend_tile(info_ref[0], query, k_ref[...], vt_ref, out_ref)


def attend(info, rows, qk, vt):
    wide, keys = vt.shape
    return pl.pallas_call(
        attend_body,
        grid_spec=pltpu.PrefetchScalarGridSpec(
            num_scalar_prefetch=1,
            grid=(rows // 256,),
            in_specs=[
                pl.BlockSpec((128, wide), lambda r, i: (i[1 + 2 * r], 0)),
                pl.BlockSpec((128, wide), lambda r, i: (i[2 + 2 * r], 0)),
                pl.BlockSpec((keys, wide), lambda r, i: (0, 1)),
                pl.BlockSpec((wide, keys), lambda r, i: (0, 0)),
            ],
            out_specs=pl.BlockSpec((wide, 256), lambda r, i: (0, r)),
        ),
        out_shape=jax.ShapeDtypeStruct((wide, rows), BF),
        compiler_params=pltpu.CompilerParams(vmem_limit_bytes=16 * 2**20),
        cost_estimate=pl.CostEstimate(
            flops=4 * rows * keys * wide, bytes_accessed=4_000_000, transcendentals=rows * keys * 3
        ),
    )(info, qk, qk, qk, vt)


def project_body(first, info_ref, own_ctx, back, ahead, far, sibling, w_hbm, own_ref, scale_ref, out_ref, w, sems):
    copies = [
        pltpu.make_async_copy(w_hbm.at[info_ref[j]], w.at[j], sems.at[j]) for j in range(8)
    ]
    for copy in copies:
        copy.start()
    near = (own_ctx, back, ahead, far)
    total = None
    for j in range(8):
        copies[j].wait()
        ctx = near[j][...] if j < 4 else sibling[j - 4]
        term = jnp.dot(w[j], ctx, preferred_element_type=F32)
        total = term if total is None else total + term
    total = scale_ref[...] * total
    for c in range(out_ref.shape[0]):
        row = lax.broadcasted_iota(jnp.int32, (1, 128), 1) + info_ref[9 + c]
        value = own_ref[first + c].astype(F32) + total[:, c * 128 : c * 128 + 128]
        out_ref[c] = jnp.where(row < info_ref[8], value, 0.0).astype(BF)


def project(first, info, near, sibling, w8, own, scale):
    chunks, tall = 4, own.shape[1]
    whole = pl.BlockSpec(memory_space=pltpu.VMEM)
    return pl.pallas_call(
        functools.partial(project_body, first),
        in_specs=[pl.BlockSpec(memory_space=pltpu.SMEM)]
        + [whole] * 5
        + [pl.BlockSpec(memory_space=pl.ANY)]
        + [whole] * 2,
        out_specs=whole,
        out_shape=jax.ShapeDtypeStruct((chunks, tall, 128), BF),
        scratch_shapes=[pltpu.VMEM(w8.shape, BF), pltpu.SemaphoreType.DMA((8,))],
        compiler_params=pltpu.CompilerParams(vmem_limit_bytes=16 * 2**20),
        cost_estimate=pl.CostEstimate(
            flops=2 * chunks * tall * 384 * 8 * 128, bytes_accessed=6_000_000, transcendentals=0
        ),
    )(info, *near, sibling, w8, own, scale)


def deliver_body(info_ref, order_ref, *refs):
    out_ref = refs[8]
    for k in range(8):
        source = (info_ref[0] - k + 8) % 8
        slot = 0
        for j in range(8):
            slot = jnp.where(order_ref[info_ref[1], j] == source, j, slot)
        out_ref[slot] = refs[k][...]


def deliver(info, order, pieces):
    whole = pl.BlockSpec(memory_space=pltpu.VMEM)
    scalars = pl.BlockSpec(memory_space=pltpu.SMEM)
    return pl.pallas_call(
        deliver_body,
        in_specs=[scalars, scalars] + [whole] * 8,
        out_specs=whole,
        out_shape=jax.ShapeDtypeStruct((8,) + pieces[0].shape, BF),
        compiler_params=pltpu.CompilerParams(vmem_limit_bytes=16 * 2**20),
    )(info, order, *pieces)


def around(x, axis, step, size):
    return lax.ppermute(x, axis, [(i, (i + step) % size) for i in range(size)])


def place(parts, places, count):
    out = jnp.zeros((count,) + parts[0].shape, parts[0].dtype)
    for part, at in zip(parts, places):
        out = lax.dynamic_update_slice(out, part[None], (at, 0, 0))
    return out.reshape(count * parts[0].shape[0], parts[0].shape[1])


def shards(images, counts, norm_gain, w_qkv, w_out, layer_scale, order):
    sec, tp, dp = (lax.axis_index(a) for a in ("section", "tp", "dp"))
    y, core = tp // 2, tp % 2
    whole = images[0]
    count = counts[0]
    share = layer_scale.shape[0]

    w_b = jnp.concatenate([w_qkv[0], w_qkv[1]], axis=1)
    block_b = lax.all_gather(w_b, "section", axis=0, tiled=False)
    own_top, own_low = block_b[:4].reshape(400, 768), block_b[4:].reshape(400, 768)

    w_o = lax.ppermute(
        w_out.T, ("section", "tp"), [(s * 8 + t, t * 8 + s) for s in range(8) for t in range(8)]
    )
    w_a = jnp.concatenate([w_qkv[2], w_o], axis=1)
    parts = (w_a, around(w_a, "dp", 1, 4), around(w_a, "dp", -1, 4), around(w_a, "dp", 2, 4))
    block_a = place(parts, (dp, (dp + 3) % 4, (dp + 1) % 4, (dp + 2) % 4), 4)
    w_v = lax.all_gather(block_a[:, :384], "section", axis=0, tiled=True)
    rel = (sec + jnp.array(ORDER, jnp.int32)) % 8
    own = lax.dynamic_slice_in_dim(whole, tp * share, share, 1)
    own = jnp.take(own.reshape(8, 128, share).transpose(0, 2, 1), rel, axis=0, mode="clip")
    normed, by_dp = normalise(whole, norm_gain)
    own_top, own_low, block_o, normed, by_dp, own = lax.optimization_barrier(
        (own_top, own_low, block_a[:, 384:], normed, by_dp, own)
    )
    w8 = lax.all_gather(block_o, "section", axis=0, tiled=False)

    back_top = around(own_top, "dp", 1, 4)
    ahead_low = around(own_low, "dp", -1, 4)
    back_low = around(own_low, "dp", 1, 4)
    ahead_top = around(own_top, "dp", -1, 4)
    far_top = around(back_top, "dp", 1, 4)
    far_low = around(ahead_low, "dp", -1, 4)

    at = jnp.stack([dp, (dp + 3) % 4, (dp + 1) % 4, (dp + 2) % 4]).astype(jnp.int32)
    at = jnp.concatenate([at, counts, rel[:4]])
    sums = early(at, by_dp, own_top, own_low, back_top, back_low, ahead_top, ahead_low)
    qk, value_t, ctx0 = late(at, sums, by_dp, far_top, far_low, normed, w_v)

    near_groups = [2 * ((y + off) % 4) + core for off in (0, 3, 1, 2)]
    far_groups = [2 * ((y + off) % 4) + 1 - core for off in (0, 3, 1, 2)]
    scale = layer_scale[:, None]

    received = {}
    info = jnp.stack(near_groups + far_groups + [count]).astype(jnp.int32)
    infos = [jnp.concatenate([info, rel[first:last] * 128]) for first, last in GROUPS]
    ask = jnp.concatenate([counts, rel[4:]])

    def both_ways(up, down):
        return around(up, "tp", 2, 8), around(down, "tp", -2, 8)

    def shared(near):
        return lax.ppermute(jnp.stack(near), "tp", [(i, i ^ 1) for i in range(8)])

    def sent(encoded, first, last):
        for j in range(first, last):
            k = ORDER[j]
            piece = encoded[j - first]
            received[k] = around(piece, "section", k, 8) if k else piece

    back0, ahead0 = both_ways(ctx0, ctx0)
    ctx1 = attend(ask, 512, qk, value_t)
    up, down = both_ways(
        jnp.concatenate([ctx1, back0[:192]], axis=0), jnp.concatenate([ctx1, ahead0[192:]], axis=0)
    )
    near0 = (ctx0, back0, ahead0, jnp.concatenate([up[384:], down[384:]], axis=0))
    back1, ahead1 = up[:384], down[:384]
    top, low = both_ways(back1[:192], ahead1[192:])
    near1 = (ctx1, back1, ahead1, jnp.concatenate([top, low], axis=0))
    sibling0 = shared(near0)
    encoded0 = project(0, infos[0], near0, sibling0, w8, own, scale)
    sent(encoded0, 0, 4)
    sibling1 = shared(near1)
    encoded1 = project(4, infos[1], near1, sibling1, w8, own, scale)
    sent(encoded1, 4, 8)
    arranged = deliver(jnp.stack([sec, dp]).astype(jnp.int32), order, [received[k] for k in range(8)])
    return arranged.transpose(0, 2, 1)[None]


def solution(mesh):
    in_specs = (
        P(("section", "dp"), None, None),
        P(("section", "dp")),
        P(),
        P(None, ("section", "dp"), "tp"),
        P("tp", ("section", "dp")),
        P("tp"),
        P(),
    )
    out_specs = P("dp", None, "section", "tp")
    return jax.shard_map(shards, mesh=mesh, in_specs=in_specs, out_specs=out_specs, check_vma=False)
```

```python
import functools
import math

import jax
import jax.numpy as jnp
from jax import lax
from jax.experimental import pallas as pl
from jax.experimental.pallas import tpu as pltpu
from jax.sharding import PartitionSpec as P

HD = 128
BF = jnp.bfloat16
F32 = jnp.float32
ORDER = (4, 3, 5, 2, 6, 1, 7, 0)


def norm_body(x_ref, gain_ref, plain, by_dp):
    x = x_ref[...].astype(F32)
    scale = lax.rsqrt(jnp.mean(x * x, axis=-1, keepdims=True) + 1e-06)
    y = (x * scale * gain_ref[...]).astype(BF)
    plain[...] = y
    for s in range(8):
        for d in range(4):
            by_dp[d, :, s * 100 : s * 100 + 100] = y[:, (s * 4 + d) * 100 : (s * 4 + d) * 100 + 100]


def normalise(x, gain):
    rows, wide = x.shape
    tile = 128
    return pl.pallas_call(
        norm_body,
        grid=(rows // tile,),
        in_specs=[
            pl.BlockSpec((tile, wide), lambda r: (r, 0)),
            pl.BlockSpec((1, wide), lambda r: (0, 0)),
        ],
        out_specs=[
            pl.BlockSpec((tile, wide), lambda r: (r, 0)),
            pl.BlockSpec((4, tile, 800), lambda r: (0, r, 0)),
        ],
        out_shape=[
            jax.ShapeDtypeStruct((rows, wide), BF),
            jax.ShapeDtypeStruct((4, rows, 800), BF),
        ],
        compiler_params=pltpu.CompilerParams(vmem_limit_bytes=16 * 2**20),
        cost_estimate=pl.CostEstimate(flops=30_000_000, bytes_accessed=20_000_000, transcendentals=1024),
    )(x, gain[None])


def early_body(at_ref, *refs):
    pairs = (len(refs) - 1) // 3
    sums, halves, out_ref = refs[: len(refs) - 1 - 3 * pairs], refs[-1 - 2 * pairs : -1], refs[-1]
    blocks = refs[len(sums) : len(sums) + pairs]
    total = sums[0][...] if sums else None
    for k in range(pairs):
        term = jnp.dot(blocks[k][0, :, :400], halves[2 * k][...], preferred_element_type=F32)
        total = term if total is None else total + term
        total += jnp.dot(blocks[k][0, :, 400:], halves[2 * k + 1][...], preferred_element_type=F32)
    out_ref[...] = total


def early(at, by_dp, sums, *halves):
    rows, deep = by_dp.shape[1:]
    wide = halves[0].shape[1]
    pairs = len(halves) // 2
    tile = rows // 4
    part = pl.BlockSpec((tile, wide), lambda r, a: (r, 0))
    blocks = [
        pl.BlockSpec((1, tile, deep), lambda r, a, k=k: (a[k], r, 0)) for k in range(pairs)
    ]
    return pl.pallas_call(
        early_body,
        grid_spec=pltpu.PrefetchScalarGridSpec(
            num_scalar_prefetch=1,
            grid=(rows // tile,),
            in_specs=[part] * len(sums)
            + blocks
            + [pl.BlockSpec((deep // 2, wide), lambda r, a: (0, 0))] * len(halves),
            out_specs=part,
        ),
        out_shape=jax.ShapeDtypeStruct((rows, wide), F32),
        compiler_params=pltpu.CompilerParams(vmem_limit_bytes=54 * 2**20),
        cost_estimate=pl.CostEstimate(
            flops=2 * pairs * rows * deep * wide, bytes_accessed=10_000_000, transcendentals=0
        ),
    )(at, *sums, *[by_dp] * pairs, *halves)


def attend_tile(live_keys, query, key, vt, out_ref):
    keys = key.shape[0]
    rows = query.shape[0]
    live = lax.broadcasted_iota(jnp.int32, (keys, rows), 0) < live_keys
    factor = math.log2(math.e) / math.sqrt(HD)
    for h in range(out_ref.shape[0] // HD):
        at = slice(h * HD, h * HD + HD)
        scores = lax.dot_general(
            key[:, at], query[:, at], (((1,), (1,)), ((), ())), preferred_element_type=F32
        )
        scores = jnp.where(live, scores, -jnp.inf)
        top = jnp.max(scores, axis=0, keepdims=True)
        expo = jnp.exp2((scores - top) * factor)
        total = jnp.sum(expo, axis=0, keepdims=True)
        context = jnp.dot(vt[at, :], expo.astype(BF), preferred_element_type=F32)
        out_ref[at, :] = (context / total).astype(BF)


def late_body(at_ref, sums, x_ref, top, low, normed, w_ref, qk_ref, vt_ref, ctx_ref, qk, vt):
    step = pl.program_id(0)
    tile, wide = sums.shape
    narrow = wide // 2

    @pl.when(step < 4)
    def _():
        total = sums[...] + jnp.dot(x_ref[0, :, :400], top[...], preferred_element_type=F32)
        total += jnp.dot(x_ref[0, :, 400:], low[...], preferred_element_type=F32)
        qk_ref[...] = total.astype(BF)
        value = jnp.dot(normed[...], w_ref[...], preferred_element_type=F32)
        vt_ref[...] = value.T.astype(BF)

    for r in range(4):

        @pl.when(step == r)
        def _():
            qk[r * tile : r * tile + tile] = qk_ref[...]
            vt[:, r * tile : r * tile + tile] = vt_ref[...]

    @pl.when(step >= 4)
    def _():
        rows = [
            pl.ds(pl.multiple_of(at_ref[5 + 2 * (step - 4) + i] * 128, 128), 128) for i in range(2)
        ]
        query = jnp.concatenate([qk[rows[0], :narrow], qk[rows[1], :narrow]], axis=0)
        attend_tile(at_ref[4], query, qk[:, narrow:], vt, ctx_ref)


def late(at, sums, by_dp, top, low, normed, w_v):
    rows, wide = sums.shape
    deep, tall = by_dp.shape[2], normed.shape[1]
    narrow = w_v.shape[1]
    tile = rows // 4
    half = pl.BlockSpec((deep // 2, wide), lambda r, a: (0, 0))

    def upto(r):
        return jnp.minimum(r, 3)

    return pl.pallas_call(
        late_body,
        grid_spec=pltpu.PrefetchScalarGridSpec(
            num_scalar_prefetch=1,
            grid=(6,),
            in_specs=[
                pl.BlockSpec((tile, wide), lambda r, a: (upto(r), 0)),
                pl.BlockSpec((1, tile, deep), lambda r, a: (a[3], upto(r), 0)),
                half,
                half,
                pl.BlockSpec((tile, tall), lambda r, a: (upto(r), 0)),
                pl.BlockSpec((tall, narrow), lambda r, a: (0, 0)),
            ],
            out_specs=[
                pl.BlockSpec((tile, wide), lambda r, a: (upto(r), 0)),
                pl.BlockSpec((narrow, tile), lambda r, a: (0, upto(r))),
                pl.BlockSpec((narrow, 256), lambda r, a: (0, jnp.maximum(r - 4, 0))),
            ],
            scratch_shapes=[pltpu.VMEM((rows, wide), BF), pltpu.VMEM((narrow, rows), BF)],
        ),
        out_shape=[
            jax.ShapeDtypeStruct((rows, wide), BF),
            jax.ShapeDtypeStruct((narrow, rows), BF),
            jax.ShapeDtypeStruct((narrow, 512), BF),
        ],
        compiler_params=pltpu.CompilerParams(vmem_limit_bytes=58 * 2**20),
        cost_estimate=pl.CostEstimate(
            flops=2 * rows * (deep * wide + tall * narrow) + 2 * rows * rows * narrow,
            bytes_accessed=18_000_000,
            transcendentals=rows * rows * 3 // 2,
        ),
    )(at, sums, by_dp, top, low, normed, w_v)


def attend_body(info_ref, q0_ref, q1_ref, k_ref, vt_ref, out_ref):
    query = jnp.concatenate([q0_ref[...], q1_ref[...]], axis=0)
    attend_tile(info_ref[0], query, k_ref[...], vt_ref, out_ref)


def attend(info, rows, qk, vt):
    wide, keys = vt.shape
    return pl.pallas_call(
        attend_body,
        grid_spec=pltpu.PrefetchScalarGridSpec(
            num_scalar_prefetch=1,
            grid=(rows // 256,),
            in_specs=[
                pl.BlockSpec((128, wide), lambda r, i: (i[1 + 2 * r], 0)),
                pl.BlockSpec((128, wide), lambda r, i: (i[2 + 2 * r], 0)),
                pl.BlockSpec((keys, wide), lambda r, i: (0, 1)),
                pl.BlockSpec((wide, keys), lambda r, i: (0, 0)),
            ],
            out_specs=pl.BlockSpec((wide, 256), lambda r, i: (0, r)),
        ),
        out_shape=jax.ShapeDtypeStruct((wide, rows), BF),
        compiler_params=pltpu.CompilerParams(vmem_limit_bytes=16 * 2**20),
        cost_estimate=pl.CostEstimate(
            flops=4 * rows * keys * wide, bytes_accessed=4_000_000, transcendentals=rows * keys * 3
        ),
    )(info, qk, qk, qk, vt)


def project_body(cuts, info_ref, *refs):
    sources, (w_hbm, mine_ref, theirs_ref, ctx, w, sems) = refs[:5], refs[5:]
    pairs = []
    for src, (first, slot, at, rows) in zip(sources, cuts):
        pairs.append((src.at[pl.ds(first, rows)], ctx.at[slot, pl.ds(at, rows)]))
    pairs += [(w_hbm.at[info_ref[j]], w.at[j]) for j in (4, 5, 6, 7, 0, 1, 2, 3)]
    copies = [pltpu.make_async_copy(*pair, sems.at[i]) for i, pair in enumerate(pairs)]
    for copy in copies:
        copy.start()
    needs = ((0,), (1,), (2,), (3, 4))
    total = None
    for j in range(4):
        for i in needs[j] + (5 + j,):
            copies[i].wait()
        term = jnp.dot(w[4 + j], ctx[j], preferred_element_type=F32)
        total = term if total is None else total + term
    theirs_ref[...] = total.astype(BF)
    total = None
    for j in range(4):
        copies[9 + j].wait()
        term = jnp.dot(w[j], ctx[j], preferred_element_type=F32)
        total = term if total is None else total + term
    mine_ref[...] = total


def project(info, parts, w8):
    tall, deep = w8.shape[1:]
    columns = parts[0][0].shape[1]
    whole = pl.BlockSpec(memory_space=pltpu.VMEM)
    return pl.pallas_call(
        functools.partial(project_body, [part[1:] for part in parts]),
        in_specs=[pl.BlockSpec(memory_space=pltpu.SMEM)] + [pl.BlockSpec(memory_space=pl.ANY)] * 6,
        out_specs=[whole, whole],
        out_shape=[
            jax.ShapeDtypeStruct((tall, columns), F32),
            jax.ShapeDtypeStruct((tall, columns), BF),
        ],
        scratch_shapes=[
            pltpu.VMEM((4, deep, columns), BF),
            pltpu.VMEM(w8.shape, BF),
            pltpu.SemaphoreType.DMA((13,)),
        ],
        compiler_params=pltpu.CompilerParams(vmem_limit_bytes=50 * 2**20),
        cost_estimate=pl.CostEstimate(
            flops=2 * columns * tall * deep * 8, bytes_accessed=6_000_000, transcendentals=0
        ),
    )(info, *[part[0] for part in parts], w8)


def finish_body(first, info_ref, mine_ref, theirs_ref, own_ref, scale_ref, *out_refs):
    for c, out_ref in enumerate(out_refs):
        at = slice(c * 128, c * 128 + 128)
        total = scale_ref[...] * (mine_ref[:, at] + theirs_ref[:, at].astype(F32))
        row = lax.broadcasted_iota(jnp.int32, (1, 128), 1) + info_ref[1 + c]
        value = own_ref[first + c].astype(F32) + total
        out_ref[...] = jnp.where(row < info_ref[0], value, 0.0).astype(BF)


def finish(first, info, mine, theirs, own, scale):
    chunks, tall = 4, own.shape[1]
    whole = pl.BlockSpec(memory_space=pltpu.VMEM)
    return pl.pallas_call(
        functools.partial(finish_body, first),
        in_specs=[pl.BlockSpec(memory_space=pltpu.SMEM)] + [whole] * 4,
        out_specs=[whole] * chunks,
        out_shape=[jax.ShapeDtypeStruct((tall, 128), BF)] * chunks,
        compiler_params=pltpu.CompilerParams(vmem_limit_bytes=24 * 2**20),
        cost_estimate=pl.CostEstimate(flops=1000, bytes_accessed=1000, transcendentals=0),
    )(info, mine, theirs, own, scale)


def deliver_body(info_ref, order_ref, *refs):
    out_ref = refs[8]
    for k in range(8):
        source = (info_ref[0] - k + 8) % 8
        slot = 0
        for j in range(8):
            slot = jnp.where(order_ref[info_ref[1], j] == source, j, slot)
        out_ref[slot] = refs[k][...]


def deliver(info, order, pieces):
    whole = pl.BlockSpec(memory_space=pltpu.VMEM)
    scalars = pl.BlockSpec(memory_space=pltpu.SMEM)
    return pl.pallas_call(
        deliver_body,
        in_specs=[scalars, scalars] + [whole] * 8,
        out_specs=whole,
        out_shape=jax.ShapeDtypeStruct((8,) + pieces[0].shape, BF),
        compiler_params=pltpu.CompilerParams(vmem_limit_bytes=16 * 2**20),
    )(info, order, *pieces)


def around(x, axis, step, size):
    return lax.ppermute(x, axis, [(i, (i + step) % size) for i in range(size)])


def place(parts, places, count):
    out = jnp.zeros((count,) + parts[0].shape, parts[0].dtype)
    for part, at in zip(parts, places):
        out = lax.dynamic_update_slice(out, part[None], (at, 0, 0))
    return out.reshape(count * parts[0].shape[0], parts[0].shape[1])


def shards(images, counts, norm_gain, w_qkv, w_out, layer_scale, order):
    sec, tp, dp = (lax.axis_index(a) for a in ("section", "tp", "dp"))
    y, core = tp // 2, tp % 2
    whole = images[0]
    count = counts[0]
    share = layer_scale.shape[0]

    w_b = jnp.concatenate([w_qkv[0], w_qkv[1]], axis=1)
    block_b = lax.all_gather(w_b, "section", axis=0, tiled=False)
    own_top, own_low = block_b[:4].reshape(400, 768), block_b[4:].reshape(400, 768)

    w_o = lax.ppermute(
        w_out.T,
        ("section", "tp"),
        [
            (s * 8 + y * 2 + c, (y * 2 + s % 2) * 8 + s // 2 * 2 + c)
            for s in range(8)
            for y in range(4)
            for c in range(2)
        ],
    )
    w_a = jnp.concatenate([w_qkv[2], w_o], axis=1)
    parts = (w_a, around(w_a, "dp", 1, 4), around(w_a, "dp", -1, 4), around(w_a, "dp", 2, 4))
    block_a = place(parts, (dp, (dp + 3) % 4, (dp + 1) % 4, (dp + 2) % 4), 4)
    w_v = lax.all_gather(block_a[:, :384], "section", axis=0, tiled=True)
    rel = (sec + jnp.array(ORDER, jnp.int32)) % 8
    own = lax.dynamic_slice_in_dim(whole, tp * share, share, 1)
    own = jnp.take(own.reshape(8, 128, share).transpose(0, 2, 1), rel, axis=0, mode="clip")
    rounds = [(y + off) % 4 * 2 for off in (0, 3, 1, 2)]
    weights_at = jnp.stack([r + core for r in rounds] + [r + 1 - core for r in rounds]).astype(jnp.int32)
    scale = jnp.broadcast_to(layer_scale[:, None], (share, 128))

    infos = [jnp.concatenate([counts, rel[first : first + 4] * 128]) for first in (0, 4)]
    ask = jnp.concatenate([counts, rel[4:]])
    at = jnp.stack([dp, (dp + 3) % 4, (dp + 1) % 4, (dp + 2) % 4]).astype(jnp.int32)
    at = jnp.concatenate([at, counts, rel[:4]])
    at_early = at[:1], at[1:3]
    place_info = jnp.stack([sec, dp]).astype(jnp.int32)
    normed, by_dp = normalise(whole, norm_gain)
    own_top, own_low, block_o, normed, by_dp, own, scale, infos, ask, at, at_early, place_info, weights_at = lax.optimization_barrier(
        (own_top, own_low, block_a[:, 384:], normed, by_dp, own, scale, infos, ask, at, at_early, place_info, weights_at)
    )
    w8 = lax.all_gather(block_o, "section", axis=0, tiled=False)

    back_top = around(own_top, "dp", 1, 4)
    ahead_low = around(own_low, "dp", -1, 4)
    back_low = around(own_low, "dp", 1, 4)
    ahead_top = around(own_top, "dp", -1, 4)
    far_top = around(back_top, "dp", 1, 4)
    far_low = around(ahead_low, "dp", -1, 4)

    sums = early(at_early[0], by_dp, (), own_top, own_low)
    sums = early(at_early[1], by_dp, (sums,), back_top, back_low, ahead_top, ahead_low)
    qk, value_t, ctx0 = late(at, sums, by_dp, far_top, far_low, normed, w_v)

    received = {}
    def both_ways(up, down):
        return around(up, "tp", 2, 8), around(down, "tp", -2, 8)

    def encoded(half, parts):
        mine, theirs = project(weights_at, parts, w8)
        theirs = lax.ppermute(theirs, "tp", [(i, i ^ 1) for i in range(8)])
        return finish(half * 4, infos[half], mine, theirs, own, scale)

    def sent(half, pieces):
        for k, piece in zip(ORDER[half * 4 : half * 4 + 4], pieces):
            received[k] = around(piece, "section", k, 8) if k else piece

    back, ahead = both_ways(ctx0, ctx0)
    ctx1 = attend(ask, 512, qk, value_t)
    up, down = both_ways(
        jnp.concatenate([ctx1, back[:192]], axis=0), jnp.concatenate([ctx1, ahead[192:]], axis=0)
    )
    top, low = both_ways(up[:192], down[192:384])
    far = ((up, 384, 3, 0, 192), (down, 384, 3, 192, 192))
    sent(0, encoded(0, ((ctx0, 0, 0, 0, 384), (back, 0, 1, 0, 384), (ahead, 0, 2, 0, 384)) + far))
    far = ((top, 0, 3, 0, 192), (low, 0, 3, 192, 192))
    sent(1, encoded(1, ((ctx1, 0, 0, 0, 384), (up, 0, 1, 0, 384), (down, 0, 2, 0, 384)) + far))
    arranged = deliver(place_info, order, [received[k] for k in range(8)])
    return arranged.transpose(0, 2, 1)[None]


def solution(mesh):
    in_specs = (
        P(("section", "dp"), None, None),
        P(("section", "dp")),
        P(),
        P(None, ("section", "dp"), "tp"),
        P("tp", ("section", "dp")),
        P("tp"),
        P(),
    )
    out_specs = P("dp", None, "section", "tp")
    return jax.shard_map(shards, mesh=mesh, in_specs=in_specs, out_specs=out_specs, check_vma=False)
```

```python
import functools
import math

import jax
import jax.numpy as jnp
from jax import lax
from jax.experimental import pallas as pl
from jax.experimental.pallas import tpu as pltpu
from jax.sharding import PartitionSpec as P

HD = 128
BF = jnp.bfloat16
F32 = jnp.float32
ORDER = (5, 3, 4, 2, 6, 7, 1, 0)


def norm_body(x_ref, gain_ref, plain, by_dp):
    x = x_ref[...].astype(F32)
    scale = lax.rsqrt(jnp.mean(x * x, axis=-1, keepdims=True) + 1e-06)
    y = (x * scale * gain_ref[...]).astype(BF)
    plain[...] = y
    for s in range(8):
        for d in range(4):
            at = s % 4 * 100
            by_dp[d * 2 + s // 4, :, at : at + 100] = y[:, (s * 4 + d) * 100 : (s * 4 + d) * 100 + 100]


def normalise(x, gain):
    rows, wide = x.shape
    tile = 128
    return pl.pallas_call(
        norm_body,
        grid=(rows // tile,),
        in_specs=[
            pl.BlockSpec((tile, wide), lambda r: (r, 0)),
            pl.BlockSpec((1, wide), lambda r: (0, 0)),
        ],
        out_specs=[
            pl.BlockSpec((tile, wide), lambda r: (r, 0)),
            pl.BlockSpec((8, tile, 400), lambda r: (0, r, 0)),
        ],
        out_shape=[
            jax.ShapeDtypeStruct((rows, wide), BF),
            jax.ShapeDtypeStruct((8, rows, 400), BF),
        ],
        compiler_params=pltpu.CompilerParams(vmem_limit_bytes=16 * 2**20),
        cost_estimate=pl.CostEstimate(flops=30_000_000, bytes_accessed=20_000_000, transcendentals=1024),
    )(x, gain[None])


def early_body(at_ref, *refs):
    pairs = (len(refs) - 1) // 3
    sums, halves, out_ref = refs[: len(refs) - 1 - 3 * pairs], refs[-1 - 2 * pairs : -1], refs[-1]
    blocks = refs[len(sums) : len(sums) + pairs]
    total = sums[0][...] if sums else None
    for k in range(pairs):
        term = jnp.dot(blocks[k][0], halves[2 * k][...], preferred_element_type=F32)
        total = term if total is None else total + term
        total += jnp.dot(blocks[k][1], halves[2 * k + 1][...], preferred_element_type=F32)
    out_ref[...] = total


def early(at, by_dp, sums, *halves):
    rows, deep = by_dp.shape[1:]
    wide = halves[0].shape[1]
    pairs = len(halves) // 2
    tile = rows // 4
    part = pl.BlockSpec((tile, wide), lambda r, a: (r, 0))
    blocks = [
        pl.BlockSpec((2, tile, deep), lambda r, a, k=k: (a[k], r, 0)) for k in range(pairs)
    ]
    return pl.pallas_call(
        early_body,
        grid_spec=pltpu.PrefetchScalarGridSpec(
            num_scalar_prefetch=1,
            grid=(rows // tile,),
            in_specs=[part] * len(sums)
            + blocks
            + [pl.BlockSpec((deep, wide), lambda r, a: (0, 0))] * len(halves),
            out_specs=part,
        ),
        out_shape=jax.ShapeDtypeStruct((rows, wide), F32),
        compiler_params=pltpu.CompilerParams(vmem_limit_bytes=40 * 2**20),
        cost_estimate=pl.CostEstimate(
            flops=4 * pairs * rows * deep * wide, bytes_accessed=10_000_000, transcendentals=0
        ),
    )(at, *sums, *[by_dp] * pairs, *halves)


def attend_tile(live_keys, query, key, vt, out_ref):
    keys = key.shape[0]
    rows = query.shape[0]
    live = lax.broadcasted_iota(jnp.int32, (keys, rows), 0) < live_keys
    factor = math.log2(math.e) / math.sqrt(HD)
    for h in range(out_ref.shape[0] // HD):
        at = slice(h * HD, h * HD + HD)
        scores = lax.dot_general(
            key[:, at], query[:, at], (((1,), (1,)), ((), ())), preferred_element_type=F32
        )
        scores = jnp.where(live, scores, -jnp.inf)
        top = jnp.max(scores, axis=0, keepdims=True)
        expo = jnp.exp2((scores - top) * factor)
        total = jnp.sum(expo, axis=0, keepdims=True)
        context = jnp.dot(vt[at, :], expo.astype(BF), preferred_element_type=F32)
        out_ref[at, :] = (context / total).astype(BF)


def late_body(at_ref, sums, x_ref, top, low, normed, w_ref, qk_ref, vt_ref, ctx_ref, qk, vt):
    step = pl.program_id(0)
    tile, wide = sums.shape
    narrow = wide // 2

    @pl.when(step < 4)
    def _():
        total = sums[...] + jnp.dot(x_ref[0], top[...], preferred_element_type=F32)
        total += jnp.dot(x_ref[1], low[...], preferred_element_type=F32)
        qk_ref[...] = total.astype(BF)
        value = jnp.dot(normed[...], w_ref[...], preferred_element_type=F32)
        vt_ref[...] = value.astype(BF).T

    for r in range(4):

        @pl.when(step == r)
        def _():
            qk[r * tile : r * tile + tile] = qk_ref[...]
            vt[:, r * tile : r * tile + tile] = vt_ref[...]

    @pl.when(step >= 4)
    def _():
        rows = [
            pl.ds(pl.multiple_of(at_ref[5 + 2 * (step - 4) + i] * 128, 128), 128) for i in range(2)
        ]
        query = jnp.concatenate([qk[rows[0], :narrow], qk[rows[1], :narrow]], axis=0)
        attend_tile(at_ref[4], query, qk[:, narrow:], vt, ctx_ref)


def late(at, sums, by_dp, top, low, normed, w_v):
    rows, wide = sums.shape
    deep, tall = by_dp.shape[2], normed.shape[1]
    narrow = w_v.shape[1]
    tile = rows // 4
    half = pl.BlockSpec((deep, wide), lambda r, a: (0, 0))

    def upto(r):
        return jnp.minimum(r, 3)

    return pl.pallas_call(
        late_body,
        grid_spec=pltpu.PrefetchScalarGridSpec(
            num_scalar_prefetch=1,
            grid=(6,),
            in_specs=[
                pl.BlockSpec((tile, wide), lambda r, a: (upto(r), 0)),
                pl.BlockSpec((2, tile, deep), lambda r, a: (a[3], upto(r), 0)),
                half,
                half,
                pl.BlockSpec((tile, tall), lambda r, a: (upto(r), 0)),
                pl.BlockSpec((tall, narrow), lambda r, a: (0, 0)),
            ],
            out_specs=[
                pl.BlockSpec((tile, wide), lambda r, a: (upto(r), 0)),
                pl.BlockSpec((narrow, tile), lambda r, a: (0, upto(r))),
                pl.BlockSpec((narrow, 256), lambda r, a: (0, jnp.maximum(r - 4, 0))),
            ],
            scratch_shapes=[pltpu.VMEM((rows, wide), BF), pltpu.VMEM((narrow, rows), BF)],
        ),
        out_shape=[
            jax.ShapeDtypeStruct((rows, wide), BF),
            jax.ShapeDtypeStruct((narrow, rows), BF),
            jax.ShapeDtypeStruct((narrow, 512), BF),
        ],
        compiler_params=pltpu.CompilerParams(vmem_limit_bytes=48 * 2**20),
        cost_estimate=pl.CostEstimate(
            flops=2 * rows * (deep * wide + tall * narrow) + 2 * rows * rows * narrow,
            bytes_accessed=18_000_000,
            transcendentals=rows * rows * 3 // 2,
        ),
    )(at, sums, by_dp, top, low, normed, w_v)


def attend_body(info_ref, q0_ref, q1_ref, k_ref, vt_ref, out_ref):
    query = jnp.concatenate([q0_ref[...], q1_ref[...]], axis=0)
    attend_tile(info_ref[0], query, k_ref[...], vt_ref, out_ref)


def attend(info, rows, qk, vt):
    wide, keys = vt.shape
    return pl.pallas_call(
        attend_body,
        grid_spec=pltpu.PrefetchScalarGridSpec(
            num_scalar_prefetch=1,
            grid=(rows // 256,),
            in_specs=[
                pl.BlockSpec((128, wide), lambda r, i: (i[1 + 2 * r], 0)),
                pl.BlockSpec((128, wide), lambda r, i: (i[2 + 2 * r], 0)),
                pl.BlockSpec((keys, wide), lambda r, i: (0, 1)),
                pl.BlockSpec((wide, keys), lambda r, i: (0, 0)),
            ],
            out_specs=pl.BlockSpec((wide, 256), lambda r, i: (0, r)),
        ),
        out_shape=jax.ShapeDtypeStruct((wide, rows), BF),
        compiler_params=pltpu.CompilerParams(vmem_limit_bytes=16 * 2**20),
        cost_estimate=pl.CostEstimate(
            flops=4 * rows * keys * wide, bytes_accessed=4_000_000, transcendentals=rows * keys * 3
        ),
    )(info, qk, qk, qk, vt)


def project_body(cuts, info_ref, *refs):
    sources, (w_hbm, mine_ref, theirs_ref, ctx, w, sems) = refs[:5], refs[5:]
    pairs = []
    for src, (first, slot, at, rows) in zip(sources, cuts):
        pairs.append((src.at[pl.ds(first, rows)], ctx.at[slot, pl.ds(at, rows)]))
    pairs += [(w_hbm.at[info_ref[j]], w.at[j]) for j in (4, 5, 6, 7, 0, 1, 2, 3)]
    copies = [pltpu.make_async_copy(*pair, sems.at[i]) for i, pair in enumerate(pairs)]
    for copy in copies:
        copy.start()
    needs = ((0,), (1,), (2,), (3, 4))
    total = None
    for j in range(4):
        for i in needs[j] + (5 + j,):
            copies[i].wait()
        term = jnp.dot(w[4 + j], ctx[j], preferred_element_type=F32)
        total = term if total is None else total + term
    theirs_ref[...] = total.astype(BF)
    total = None
    for j in range(4):
        copies[9 + j].wait()
        term = jnp.dot(w[j], ctx[j], preferred_element_type=F32)
        total = term if total is None else total + term
    mine_ref[...] = total


def project(info, parts, w8):
    tall, deep = w8.shape[1:]
    columns = parts[0][0].shape[1]
    whole = pl.BlockSpec(memory_space=pltpu.VMEM)
    return pl.pallas_call(
        functools.partial(project_body, [part[1:] for part in parts]),
        in_specs=[pl.BlockSpec(memory_space=pltpu.SMEM)] + [pl.BlockSpec(memory_space=pl.ANY)] * 6,
        out_specs=[whole, whole],
        out_shape=[
            jax.ShapeDtypeStruct((tall, columns), F32),
            jax.ShapeDtypeStruct((tall, columns), BF),
        ],
        scratch_shapes=[
            pltpu.VMEM((4, deep, columns), BF),
            pltpu.VMEM(w8.shape, BF),
            pltpu.SemaphoreType.DMA((13,)),
        ],
        compiler_params=pltpu.CompilerParams(vmem_limit_bytes=50 * 2**20),
        cost_estimate=pl.CostEstimate(
            flops=2 * columns * tall * deep * 8, bytes_accessed=6_000_000, transcendentals=0
        ),
    )(info, *[part[0] for part in parts], w8)


def finish_body(first, info_ref, mine_ref, theirs_ref, own_ref, scale_ref, *out_refs):
    for c, out_ref in enumerate(out_refs):
        at = slice(c * 128, c * 128 + 128)
        total = scale_ref[...] * (mine_ref[:, at] + theirs_ref[:, at].astype(F32))
        row = lax.broadcasted_iota(jnp.int32, (1, 128), 1) + info_ref[1 + c]
        value = own_ref[first + c].astype(F32) + total
        out_ref[...] = jnp.where(row < info_ref[0], value, 0.0).astype(BF)


def finish(first, info, mine, theirs, own, scale):
    chunks, tall = 4, own.shape[1]
    whole = pl.BlockSpec(memory_space=pltpu.VMEM)
    return pl.pallas_call(
        functools.partial(finish_body, first),
        in_specs=[pl.BlockSpec(memory_space=pltpu.SMEM)] + [whole] * 4,
        out_specs=[whole] * chunks,
        out_shape=[jax.ShapeDtypeStruct((tall, 128), BF)] * chunks,
        compiler_params=pltpu.CompilerParams(vmem_limit_bytes=24 * 2**20),
        cost_estimate=pl.CostEstimate(flops=1000, bytes_accessed=1000, transcendentals=0),
    )(info, mine, theirs, own, scale)


def deliver_body(info_ref, order_ref, *refs):
    out_ref = refs[8]
    for i, k in enumerate(ORDER[::-1]):
        source = (info_ref[0] - k + 8) % 8
        slot = 0
        for j in range(8):
            slot = jnp.where(order_ref[info_ref[1], j] == source, j, slot)
        out_ref[slot] = refs[i][...]


def deliver(info, order, pieces):
    whole = pl.BlockSpec(memory_space=pltpu.VMEM)
    scalars = pl.BlockSpec(memory_space=pltpu.SMEM)
    return pl.pallas_call(
        deliver_body,
        in_specs=[scalars, scalars] + [whole] * 8,
        out_specs=whole,
        out_shape=jax.ShapeDtypeStruct((8,) + pieces[0].shape, BF),
        compiler_params=pltpu.CompilerParams(vmem_limit_bytes=16 * 2**20),
    )(info, order, *pieces)


def around(x, axis, step, size):
    return lax.ppermute(x, axis, [(i, (i + step) % size) for i in range(size)])


def place(parts, places, count):
    out = jnp.zeros((count,) + parts[0].shape, parts[0].dtype)
    for part, at in zip(parts, places):
        out = lax.dynamic_update_slice(out, part[None], (at, 0, 0))
    return out.reshape(count * parts[0].shape[0], parts[0].shape[1])


def shards(images, counts, norm_gain, w_qkv, w_out, layer_scale, order):
    sec, tp, dp = (lax.axis_index(a) for a in ("section", "tp", "dp"))
    y, core = tp // 2, tp % 2
    whole = images[0]
    count = counts[0]
    share = layer_scale.shape[0]

    w_b = jnp.concatenate([w_qkv[0], w_qkv[1]], axis=1)
    block_b = lax.all_gather(w_b, "section", axis=0, tiled=False)
    own_top, own_low = block_b[:4].reshape(400, 768), block_b[4:].reshape(400, 768)

    w_o = lax.ppermute(
        w_out.T,
        ("section", "tp"),
        [
            (s * 8 + y * 2 + c, (y * 2 + s % 2) * 8 + s // 2 * 2 + c)
            for s in range(8)
            for y in range(4)
            for c in range(2)
        ],
    )
    w_a = jnp.concatenate([w_qkv[2], w_o], axis=1)
    parts = (w_a, around(w_a, "dp", 1, 4), around(w_a, "dp", -1, 4), around(w_a, "dp", 2, 4))
    block_a = place(parts, (dp, (dp + 3) % 4, (dp + 1) % 4, (dp + 2) % 4), 4)
    w_v = lax.all_gather(block_a[:, :384], "section", axis=0, tiled=True)
    rel = (sec + jnp.array(ORDER, jnp.int32)) % 8
    own = lax.dynamic_slice_in_dim(whole, tp * share, share, 1)
    own = jnp.take(own.reshape(8, 128, share).transpose(0, 2, 1), rel, axis=0, mode="clip")
    rounds = [(y + off) % 4 * 2 for off in (0, 3, 1, 2)]
    weights_at = jnp.stack([r + core for r in rounds] + [r + 1 - core for r in rounds]).astype(jnp.int32)
    scale = jnp.broadcast_to(layer_scale[:, None], (share, 128))

    infos = [jnp.concatenate([counts, rel[first : first + 4] * 128]) for first in (0, 4)]
    ask = jnp.concatenate([counts, rel[4:]])
    at = jnp.stack([dp, (dp + 3) % 4, (dp + 1) % 4, (dp + 2) % 4]).astype(jnp.int32)
    at = jnp.concatenate([at, counts, rel[:4]])
    at_early = at[:1], at[1:3]
    place_info = jnp.stack([sec, dp]).astype(jnp.int32)
    normed, by_dp = normalise(whole, norm_gain)
    own_top, own_low, block_o, normed, by_dp, own, scale, infos, ask, at, at_early, place_info, weights_at = lax.optimization_barrier(
        (own_top, own_low, block_a[:, 384:], normed, by_dp, own, scale, infos, ask, at, at_early, place_info, weights_at)
    )
    w8 = lax.all_gather(block_o, "section", axis=0, tiled=False)

    back_top = around(own_top, "dp", 1, 4)
    ahead_low = around(own_low, "dp", -1, 4)
    back_low = around(own_low, "dp", 1, 4)
    ahead_top = around(own_top, "dp", -1, 4)
    far_top = around(back_top, "dp", 1, 4)
    far_low = around(ahead_low, "dp", -1, 4)

    sums = early(at_early[0], by_dp, (), own_top, own_low)
    sums = early(at_early[1], by_dp, (sums,), back_top, back_low, ahead_top, ahead_low)
    qk, value_t, ctx0 = late(at, sums, by_dp, far_top, far_low, normed, w_v)

    received = {}
    def both_ways(up, down):
        return around(up, "tp", 2, 8), around(down, "tp", -2, 8)

    def encoded(half, parts):
        mine, theirs = project(weights_at, parts, w8)
        theirs = lax.ppermute(theirs, "tp", [(i, i ^ 1) for i in range(8)])
        return finish(half * 4, infos[half], mine, theirs, own, scale)

    def sent(half, pieces):
        for k, piece in zip(ORDER[half * 4 : half * 4 + 4], pieces):
            received[k] = around(piece, "section", k, 8) if k else piece

    back, ahead = both_ways(ctx0, ctx0)
    ctx1 = attend(ask, 512, qk, value_t)
    up, down = both_ways(
        jnp.concatenate([ctx1, back[:192]], axis=0), jnp.concatenate([ctx1, ahead[192:]], axis=0)
    )
    top, low = both_ways(up[:192], down[192:384])
    far = ((up, 384, 3, 0, 192), (down, 384, 3, 192, 192))
    sent(0, encoded(0, ((ctx0, 0, 0, 0, 384), (back, 0, 1, 0, 384), (ahead, 0, 2, 0, 384)) + far))
    far = ((top, 0, 3, 0, 192), (low, 0, 3, 192, 192))
    sent(1, encoded(1, ((ctx1, 0, 0, 0, 384), (up, 0, 1, 0, 384), (down, 0, 2, 0, 384)) + far))
    arranged = deliver(place_info, order, [received[k] for k in ORDER[::-1]])
    return arranged.transpose(0, 2, 1)[None]


def solution(mesh):
    in_specs = (
        P(("section", "dp"), None, None),
        P(("section", "dp")),
        P(),
        P(None, ("section", "dp"), "tp"),
        P("tp", ("section", "dp")),
        P("tp"),
        P(),
    )
    out_specs = P("dp", None, "section", "tp")
    return jax.shard_map(shards, mesh=mesh, in_specs=in_specs, out_specs=out_specs, check_vma=False)
```
